32 devices in a mesh: dp: 8 (over z, x), expert: 4 (over y, core).
Axes of the slice: x: 2, y: 2, z: 4, core: 2. Of those that a mesh axis runs over, the one named last changes fastest.
Arguments:
- momentum: float32 [4, 16384, 512], P(None, ('dp', 'expert')), may hold values from -6 to 6
- gradient: bfloat16 [4, 16384, 512], P(None, ('dp', 'expert')), may hold values from -6 to 6
- weights: float32 [4, 16384, 512], P(None, ('dp', 'expert')), may hold values from -0.25 to 0.25
- logit_max: int32 [4, 64], replicated, may hold values from 50 to 799
- clip_flag: int32 [4, 64], replicated, may hold values 0 or 1
Outputs:
- new_weights: float32 [4, 16384, 512], P(None, ('dp', 'expert'))
- new_momentum: float32 [4, 16384, 512], P(None, ('dp', 'expert'))
The draws below stay inside these ranges and needn't reach their ends.
All inputs are finite; a program needn't handle non-finite values.
Results may differ from the reference program's by a relative error of at most 0.0003.
Values sent between devices are 32-bit elements; how exact they have to be, the bound alone decides.
A program may use at most 128 MiB of HBM per device.

```python
import math
import jax
import jax.numpy as jnp
from jax import lax

HEADS = 64
NOPE = 128
VDIM = 128
LATENT = 512
ITERS = 3
ROWS = 16384
MATS = 4


def set_ends(values, stream_key, smallest, top_value):
    index_at = [jax.random.randint(jax.random.fold_in(stream_key, axis), (), 0, length) for axis, length in enumerate(values.shape)]
    main_axis = values.shape.index(max(values.shape))
    next_to = index_at[:main_axis] + [(index_at[main_axis] + 1) % values.shape[main_axis]] + index_at[main_axis + 1:]
    return values.at[tuple(index_at)].set(smallest).at[tuple(next_to)].set(top_value)


def block_levels(stream_key, extent, cuts, smallest, largest):
    def one(axis_at, shards_of):
        steps = jax.random.uniform(jax.random.fold_in(jax.random.fold_in(stream_key, 6), axis_at), (shards_of,), jnp.float32, smallest / len(cuts), largest / len(cuts))
        return jnp.repeat(jnp.exp(steps), extent[axis_at] // shards_of).reshape((-1,) + (1,) * (len(extent) - axis_at - 1))

    loudness = one(*cuts[0])
    for cut in cuts[1:]:
        loudness = loudness * one(*cut)
    return loudness


def scatter_about(key, extent, scale, bound, shards=(), kind=jnp.bfloat16):
    result = jax.random.normal(key, extent, jnp.float32) * scale
    if len(shards) > 0:
        result = block_levels(key, extent, shards, -0.22, 0.18) * result
    return jnp.clip(result, min=-bound, max=bound).astype(kind)


def setup_inputs(seed: int = 0) -> dict:
    key_of = jax.random.split(jax.random.key(seed), 6)
    momentum = scatter_about(key_of[0], (MATS, ROWS, LATENT), 1.0, 6.0, ((1, 32),), jnp.float32)
    gradient = scatter_about(key_of[1], (MATS, ROWS, LATENT), 1.0, 6.0, ((1, 32),))
    weights = scatter_about(key_of[2], (MATS, ROWS, LATENT), LATENT ** -0.5, 0.25, ((1, 32),), jnp.float32)
    logit_max = set_ends(jax.random.randint(key_of[3], (MATS, HEADS), 50, 800), jax.random.fold_in(key_of[3], 1), 50, 799).astype(jnp.int32)
    clip_flag = set_ends((jax.random.randint(key_of[4], (MATS, HEADS), 0, 2) < 1).astype(jnp.int32), jax.random.fold_in(key_of[4], 1), 0, 1)
    return {"momentum": momentum, "gradient": gradient, "weights": weights, "logit_max": logit_max, "clip_flag": clip_flag}


highest = lax.Precision.HIGHEST
momentum_decay = 0.95
learn_rate = 0.2
weight_decay = 0.1
epsilon = 1e-07
clip_tau = 100.0
coeff_a = 3.4445
coeff_b = -4.775
coeff_c = 2.0315

def orthogonal(matrix):
    norm_value = jnp.sqrt(jnp.sum(matrix * matrix))
    current = matrix / (norm_value + epsilon)
    for step in range(ITERS):
        gram_matrix = jnp.dot(current.T, current, precision=highest, preferred_element_type=jnp.float32)
        square = jnp.dot(gram_matrix, gram_matrix, precision=highest, preferred_element_type=jnp.float32)
        poly = coeff_b * gram_matrix + coeff_c * square
        current = coeff_a * current + jnp.dot(current, poly, precision=highest, preferred_element_type=jnp.float32)
    return current

def reference(momentum, gradient, weights, logit_max, clip_flag):
    new_momentum = momentum_decay * momentum + gradient.astype(jnp.float32)
    ortho = lax.map(orthogonal, new_momentum)
    update_scale = 0.2 * math.sqrt(max(ROWS, LATENT))
    stepped = weights - learn_rate * (update_scale * ortho + weight_decay * weights)
    gamma = jnp.where(clip_flag == 1, jnp.minimum(1.0, clip_tau / logit_max.astype(jnp.float32)), 1.0)
    root = jnp.sqrt(gamma)
    head_span = NOPE + VDIM
    row_root = jnp.repeat(root, head_span, axis=1)
    position = jnp.arange(ROWS) % head_span
    factor = jnp.where(position[None, :] < NOPE, row_root, 1.0)
    new_weights = stepped * factor[:, :, None]
    return (new_weights, new_momentum)
```

```python
import math

import jax
import jax.numpy as jnp
from jax import lax
from jax.sharding import PartitionSpec as P

HEADS = 64
NOPE = 128
VDIM = 128
LATENT = 512
ITERS = 3
ROWS = 16384


high = lax.Precision.HIGH
momentum_decay = 0.95
learn_rate = 0.2
weight_decay = 0.1
epsilon = 1e-07
clip_tau = 100.0
coeff_a = 3.4445
coeff_b = -4.775
coeff_c = 2.0315


def product_of(left, right):
    return jnp.matmul(left, right, precision=high, preferred_element_type=jnp.float32)


def chain_of(gram):
    identity = jnp.eye(gram.shape[-1], dtype=jnp.float32)
    product = None
    for step in range(ITERS):
        factor = coeff_a * identity + coeff_b * gram + coeff_c * product_of(gram, gram)
        product = factor if product is None else product_of(product, factor)
        if step + 1 < ITERS:
            gram = product_of(factor, product_of(gram, factor))
    return product


def body(momentum, gradient, weights, logit_max, clip_flag):
    new_momentum = momentum_decay * momentum + gradient.astype(jnp.float32)
    partial = jnp.einsum(
        "mri,mrj->mij", new_momentum, new_momentum, precision=high, preferred_element_type=jnp.float32
    )
    gram = lax.psum_scatter(partial, "expert", scatter_dimension=0, tiled=True)
    gram = lax.psum(gram, "dp")
    squares = jnp.trace(gram, axis1=1, axis2=2)
    inverse = (1.0 / (jnp.sqrt(squares) + epsilon))[:, None, None]
    product = inverse * chain_of(gram * inverse * inverse)
    product = lax.all_gather(product, "expert", axis=0, tiled=True)
    ortho = product_of(new_momentum, product)
    update_scale = 0.2 * math.sqrt(max(ROWS, LATENT))
    stepped = weights - learn_rate * (update_scale * ortho + weight_decay * weights)
    gamma = jnp.where(
        clip_flag == 1, jnp.minimum(1.0, clip_tau / logit_max.astype(jnp.float32)), 1.0
    )
    root = jnp.sqrt(gamma)
    local_rows = weights.shape[1]
    block_index = lax.axis_index("dp") * lax.axis_size("expert") + lax.axis_index("expert")
    row_index = block_index * local_rows + lax.iota(jnp.int32, local_rows)
    head_span = NOPE + VDIM
    head_of = row_index // head_span
    onehot = (head_of[:, None] == lax.iota(jnp.int32, HEADS)[None, :]).astype(jnp.float32)
    row_root = jnp.dot(root, onehot.T, precision=lax.Precision.HIGHEST, preferred_element_type=jnp.float32)
    factor = jnp.where((row_index % head_span < NOPE)[None, :], row_root, 1.0)
    new_weights = stepped * factor[:, :, None]
    return (new_weights, new_momentum)


def solution(mesh):
    return jax.shard_map(
        body,
        mesh=mesh,
        in_specs=(
            P(None, ("dp", "expert"), None),
            P(None, ("dp", "expert"), None),
            P(None, ("dp", "expert"), None),
            P(),
            P(),
        ),
        out_specs=(P(None, ("dp", "expert"), None), P(None, ("dp", "expert"), None)),
        check_vma=False,
    )
```

```python
import math

import jax
import jax.numpy as jnp
from jax import lax
from jax.experimental import pallas as pl
from jax.experimental.pallas import tpu as pltpu
from jax.sharding import PartitionSpec as P

HEADS = 64
NOPE = 128
VDIM = 128
LATENT = 512
ITERS = 3
ROWS = 16384

momentum_decay = 0.95
learn_rate = 0.2
weight_decay = 0.1
epsilon = 1e-07
clip_tau = 100.0
coeff_a = 3.4445
coeff_b = -4.775
coeff_c = 2.0315

MESH = pl.DeviceIdType.MESH
f32 = jnp.float32
bf16 = jnp.bfloat16
HALF = LATENT // 2
PACK = 3 * HALF
SHARE = PACK // 2
PART = SHARE // 2
CHUNKS = 4
PIECE = SHARE // CHUNKS


def halves(value):
    high = value.astype(bf16)
    return high, (value - high.astype(f32)).astype(bf16)


def dot(left, right):
    return jnp.dot(left, right, preferred_element_type=f32)


def dot_t(left, right):
    return lax.dot_general(left, right, (((1,), (1,)), ((), ())), preferred_element_type=f32)


def dot3(left, right, dot=dot):
    return dot(left[0], right[0]) + (dot(left[0], right[1]) + dot(left[1], right[0]))


def flipped(index, weight):
    bit = (index // weight) % 2
    return index + weight * (1 - 2 * bit), bit


def chain(gsum, ga, gb, q_ref, hi, lo):
    row = lax.broadcasted_iota(jnp.int32, (HALF, HALF), 0)
    col = lax.broadcasted_iota(jnp.int32, (HALF, HALF), 1)
    eye = (row == col).astype(f32)
    g00 = gsum[0:HALF]
    g01 = gsum[HALF : 2 * HALF]
    g11 = gsum[2 * HALF : PACK]
    squares = jnp.sum((g00 + g11) * eye, keepdims=True)
    inverse = 1.0 / (jnp.sqrt(squares) + epsilon)
    inv2 = inverse * inverse

    def put(slot, rows, cols, value):
        high, low = halves(value)
        hi[slot, rows, cols] = high
        lo[slot, rows, cols] = low

    first, second = slice(0, HALF), slice(HALF, LATENT)
    whole = slice(0, LATENT)
    g01 = g01 * inv2
    for rows, cols, value in (
        (first, first, g00 * inv2),
        (first, second, g01),
        (second, first, g01.T),
        (second, second, g11 * inv2),
    ):
        ga[rows, cols] = value
        put(0, rows, cols, value)

    def times(left, right, cols):
        return dot3((hi[left], lo[left]), (hi[right, :, cols], lo[right, :, cols]))

    row = lax.broadcasted_iota(jnp.int32, (LATENT, HALF), 0)
    col = lax.broadcasted_iota(jnp.int32, (LATENT, HALF), 1)
    diagonal = {0: (row == col).astype(f32) * coeff_a, 1: (row == col + HALF).astype(f32) * coeff_a}
    for step in range(ITERS):
        factor_slot = 3 if step == 0 else 1
        for index, cols in enumerate((first, second)):
            factor = diagonal[index] + coeff_b * ga[:, cols] + coeff_c * times(0, 0, cols)
            put(factor_slot, whole, cols, factor)
        if step + 1 < ITERS:
            for cols in (first, second):
                put(2, whole, cols, times(0, factor_slot, cols))
            for cols in (first, second):
                value = times(factor_slot, 2, cols)
                ga[:, cols] = value
                put(0, whole, cols, value)
        if 0 < step < ITERS - 1:
            for cols in (first, second):
                gb[:, cols] = times(3, 1, cols)
            for cols in (first, second):
                put(3, whole, cols, gb[:, cols])
    q_ref[0:HALF] = inverse * dot3((hi[3, first], lo[3, first]), (hi[1, :, first], lo[1, :, first]))
    right = times(3, 1, second)
    q_ref[HALF:PACK] = inverse * right


def exchange_kernel(
    n_dp, n_ex, m_any, g_any, out_a, out_b,
    m_buf, g_buf, gram, from_core, buf_a, buf_b, rec_a, rec_b,
    z_own, z_left, z_right, s_left, s_right, gsum, packed, ga, gb, hi, lo,
    load_sem, core_send, core_recv, plane_send, plane_recv, z_send, z_recv, sum_send, sum_recv,
    back_send, back_recv, last_send, last_recv,
):
    mats = m_buf.shape[0]
    n_y = n_ex // 2
    steps = mats.bit_length() - 1
    d, e = lax.axis_index("dp"), lax.axis_index("expert")
    mate, core = flipped(e, 1)
    other_x, x_bit = flipped(d, 1)
    here, line = d // 2, n_dp // 2
    y = e // 2

    for k in range(mats):
        pltpu.make_async_copy(m_any.at[k], m_buf.at[k], load_sem.at[k, 0]).start()
        pltpu.make_async_copy(g_any.at[k], g_buf.at[k], load_sem.at[k, 1]).start()

    y_bits = []
    weight = n_y // 2
    while weight >= 1:
        partner, bit = flipped(e, 2 * weight)
        y_bits.append(({"expert": partner}, bit))
        weight //= 2
    x_entry = ({"dp": other_x}, x_bit)
    order_a, order_b = [x_entry] + y_bits, y_bits + [x_entry]

    barrier = pltpu.get_barrier_semaphore()
    pl.semaphore_signal(barrier, inc=1, device_id={"expert": mate}, device_id_type=MESH)
    for partner, _ in order_a:
        pl.semaphore_signal(barrier, inc=1, device_id=partner, device_id_type=MESH)

    @pl.when(here > 0)
    def _():
        pl.semaphore_signal(barrier, inc=1, device_id={"dp": d - 2}, device_id_type=MESH)

    @pl.when(here < line - 1)
    def _():
        pl.semaphore_signal(barrier, inc=1, device_id={"dp": d + 2}, device_id_type=MESH)

    ends = (here > 0).astype(jnp.int32) + (here < line - 1).astype(jnp.int32)
    pl.semaphore_wait(barrier, 1 + steps + ends)

    def core_copy(k):
        return pltpu.make_async_remote_copy(
            src_ref=gram.at[k, pl.ds((1 - core) * SHARE, SHARE)],
            dst_ref=from_core.at[k],
            send_sem=core_send.at[k],
            recv_sem=core_recv.at[k],
            device_id={"expert": mate},
            device_id_type=MESH,
        )

    @pl.loop(0, mats)
    def _(k):
        pltpu.make_async_copy(m_any.at[k], m_buf.at[k], load_sem.at[k, 0]).wait()
        pltpu.make_async_copy(g_any.at[k], g_buf.at[k], load_sem.at[k, 1]).wait()
        moved = momentum_decay * m_buf[k] + g_buf[k].astype(f32)
        high, low = halves(moved)
        high_t, low_t = halves(moved.T)
        for at, (i, j) in enumerate(((0, 0), (0, 1), (1, 1))):
            rows, cols = slice(i * HALF, (i + 1) * HALF), slice(j * HALF, (j + 1) * HALF)
            gram[k, at * HALF : (at + 1) * HALF] = dot3(
                (high_t[rows], low_t[rows]), (high[:, cols], low[:, cols])
            )
        core_copy(k).start()

    @pl.loop(0, mats)
    def _(k):
        core_copy(k).wait()
        swapped = (k % n_y) * 2 + k // n_y
        start = pl.multiple_of(core * SHARE, SHARE)
        buf_a[k] = gram[k, pl.ds(start, PART)] + from_core[k, 0:PART]
        buf_b[swapped] = gram[k, pl.ds(start + PART, PART)] + from_core[k, PART:SHARE]

    at_a = at_b = 0
    count, offset = mats, 0
    for step in range(steps):
        count //= 2
        copies = []
        for side, (buf, rec, order, at) in enumerate(
            ((buf_a, rec_a, order_a, at_a), (buf_b, rec_b, order_b, at_b))
        ):
            partner, bit = order[step]
            copy = pltpu.make_async_remote_copy(
                src_ref=buf.at[pl.ds(at + (1 - bit) * count, count)],
                dst_ref=rec.at[pl.ds(offset, count)],
                send_sem=plane_send.at[side, step],
                recv_sem=plane_recv.at[side, step],
                device_id=partner,
                device_id_type=MESH,
            )
            copy.start()
            copies.append(copy)
        at_a = at_a + order_a[step][1] * count
        at_b = at_b + order_b[step][1] * count
        for copy, buf, rec, at in zip(copies, (buf_a, buf_b), (rec_a, rec_b), (at_a, at_b)):
            copy.wait()
            for i in range(count):
                buf[at + i] = buf[at + i] + rec[offset + i]
        offset += count

    per = CHUNKS // 2
    for c in range(CHUNKS):
        source, at = (buf_a, at_a) if c < per else (buf_b, at_b)
        z_own[c] = source[at, (c % per) * PIECE : (c % per + 1) * PIECE]

    @pl.when(here == 0)
    def _():
        z_left[...] = jnp.zeros_like(z_left)

    @pl.when(here == line - 1)
    def _():
        z_right[...] = jnp.zeros_like(z_right)

    def line_copy(way, c):
        source, target = ((s_left, z_left), (s_right, z_right))[way]
        return pltpu.make_async_remote_copy(
            src_ref=source.at[c],
            dst_ref=target.at[c],
            send_sem=z_send.at[way, c],
            recv_sem=z_recv.at[way, c],
            device_id={"dp": d + 2 if way == 0 else d - 2},
            device_id_type=MESH,
        )

    def sum_copy(c):
        rows = pl.ds(pl.multiple_of(core * SHARE + c * PIECE, PIECE), PIECE)
        return pltpu.make_async_remote_copy(
            src_ref=gsum.at[rows],
            dst_ref=gsum.at[rows],
            send_sem=sum_send.at[c],
            recv_sem=sum_recv.at[c],
            device_id={"expert": mate},
            device_id_type=MESH,
        )

    there = line - 1 - here
    far = jnp.maximum(here, there)

    @pl.loop(0, line + CHUNKS - 1)
    def _(t):
        for way, behind in ((0, here), (1, there)):
            source, target = ((s_left, z_left), (s_right, z_right))[way]
            c = t - behind

            @pl.when((c >= 0) & (c < CHUNKS))
            def _():
                @pl.when(behind > 0)
                def _():
                    line_copy(way, c).wait_recv()

                @pl.when(behind < line - 1)
                def _():
                    source[c] = target[c] + z_own[c]
                    line_copy(way, c).start()

        c = t - far

        @pl.when((c >= 0) & (c < CHUNKS))
        def _():
            rows = pl.ds(pl.multiple_of(core * SHARE + c * PIECE, PIECE), PIECE)
            gsum[rows] = (z_left[c] + z_own[c]) + z_right[c]
            sum_copy(c).start()

    @pl.loop(0, CHUNKS)
    def _(c):
        sum_copy(c).wait()

        @pl.when(here < line - 1)
        def _():
            line_copy(0, c).wait_send()

        @pl.when(here > 0)
        def _():
            line_copy(1, c).wait_send()

    chain(gsum, ga, gb, packed, hi, lo)

    own_rows = pl.multiple_of(core * SHARE, SHARE)
    out_a[core, at_a] = packed[pl.ds(own_rows, PART)]
    out_b[core, at_b] = packed[pl.ds(own_rows + PART, PART)]
    count = 1
    pending = []
    news = [(out_a, at_a), (out_b, at_b)]
    starts = [at_a, at_b]
    orders = [order_a, order_b]
    for step in range(steps + 1):
        copies = []
        if step < steps:
            for side, buf in enumerate((out_a, out_b)):
                partner, bit = orders[side][steps - 1 - step]
                block = buf.at[core, pl.ds(starts[side], count)]
                copy = pltpu.make_async_remote_copy(
                    src_ref=block, dst_ref=block,
                    send_sem=back_send.at[side, step], recv_sem=back_recv.at[side, step],
                    device_id=partner, device_id_type=MESH,
                )
                copy.start()
                copies.append(copy)
        fresh = count // 2 if step > 0 else 1
        for side, (buf, at) in enumerate(news):
            block = buf.at[core, pl.ds(at, fresh)]
            copy = pltpu.make_async_remote_copy(
                src_ref=block, dst_ref=block,
                send_sem=last_send.at[side, step], recv_sem=last_recv.at[side, step],
                device_id={"expert": mate}, device_id_type=MESH,
            )
            copy.start()
            pending.append(copy)
        if step < steps:
            news = []
            for side, buf in enumerate((out_a, out_b)):
                copies[side].wait()
                bit = orders[side][steps - 1 - step][1]
                news.append((buf, starts[side] + (1 - 2 * bit) * count))
                starts[side] = starts[side] - bit * count
            count *= 2
    for copy in pending:
        copy.wait()


def exchange(momentum, gradient, n_dp, n_ex):
    mats, rows, width = momentum.shape
    steps = mats.bit_length() - 1
    dma = pltpu.SemaphoreType.DMA
    kernel = lambda *refs: exchange_kernel(n_dp, n_ex, *refs)
    result = jax.ShapeDtypeStruct((2, mats, PART, HALF), f32)
    return pl.pallas_call(
        kernel,
        out_shape=(result, result),
        in_specs=[pl.BlockSpec(memory_space=pl.ANY)] * 2,
        out_specs=[pl.BlockSpec(memory_space=pltpu.VMEM)] * 2,
        scratch_shapes=[
            pltpu.VMEM((mats, rows, width), f32),
            pltpu.VMEM((mats, rows, width), bf16),
            pltpu.VMEM((mats, PACK, HALF), f32),
            pltpu.VMEM((mats, SHARE, HALF), f32),
            pltpu.VMEM((mats, PART, HALF), f32),
            pltpu.VMEM((mats, PART, HALF), f32),
            pltpu.VMEM((mats, PART, HALF), f32),
            pltpu.VMEM((mats, PART, HALF), f32),
        ]
        + [pltpu.VMEM((CHUNKS, PIECE, HALF), f32)] * 5
        + [pltpu.VMEM((PACK, HALF), f32)] * 2
        + [pltpu.VMEM((width, width), f32)] * 2
        + [pltpu.VMEM((4, width, width), bf16)] * 2
        + [dma((mats, 2)), dma((mats,)), dma((mats,))]
        + [dma((2, steps))] * 2
        + [dma((2, CHUNKS))] * 2
        + [dma((CHUNKS,))] * 2
        + [dma((2, steps))] * 2
        + [dma((2, steps + 1))] * 2,
        compiler_params=pltpu.CompilerParams(
            collective_id=0, has_side_effects=True, vmem_limit_bytes=56 * 2**20
        ),
        name="exchange",
    )(momentum, gradient)


def update_kernel(
    span, local_rows, n_ex, logit_ref, flag_ref, m_ref, g_ref, w_ref, a_ref, b_ref, w_out, m_out,
):
    k, tile = pl.program_id(0), pl.program_id(1)
    rows = m_ref.shape[1]
    moved = momentum_decay * m_ref[0] + g_ref[0].astype(f32)
    m_out[0] = moved
    high, low = halves(moved)
    pack = jnp.concatenate([a_ref[0, 0], b_ref[0, 0], a_ref[1, 0], b_ref[1, 0]], axis=0)
    pack_hi, pack_lo = halves(pack)
    p00, p01, p11 = [
        (pack_hi[i * HALF : (i + 1) * HALF], pack_lo[i * HALF : (i + 1) * HALF]) for i in range(3)
    ]
    x0 = (high[:, :HALF], low[:, :HALF])
    x1 = (high[:, HALF:], low[:, HALF:])
    ortho = (dot3(x0, p00) + dot3(x1, p01, dot_t), dot3(x0, p01) + dot3(x1, p11))
    update_scale = 0.2 * math.sqrt(max(ROWS, LATENT))
    first = (lax.axis_index("dp") * n_ex + lax.axis_index("expert")) * local_rows + tile * rows
    for i in range(rows // span):
        row = first + i * span
        head = row // (NOPE + VDIM)
        logit = jnp.full((1, HALF), logit_ref[k, head], jnp.int32).astype(f32)
        use = jnp.full((1, HALF), flag_ref[k, head], jnp.int32) == 1
        keyed = jnp.full((1, HALF), row % (NOPE + VDIM), jnp.int32) < NOPE
        root = jnp.sqrt(jnp.minimum(1.0, clip_tau / logit))
        factor = jnp.where(use & keyed, root, 1.0)
        at = slice(i * span, (i + 1) * span)
        for j in range(2):
            cols = slice(j * HALF, (j + 1) * HALF)
            weight = w_ref[0, at, cols]
            stepped = weight - learn_rate * (
                update_scale * ortho[j][at] + weight_decay * weight
            )
            w_out[0, at, cols] = stepped * factor


def update(momentum, gradient, weights, logit_max, clip_flag, part_a, part_b, n_ex):
    mats, local_rows, width = momentum.shape
    rows = min(local_rows, 256)
    span = min(rows, NOPE)
    n_y = n_ex // 2
    block = pl.BlockSpec((1, rows, width), lambda k, i: (k, i, 0))
    scalar = pl.BlockSpec(memory_space=pltpu.SMEM)
    result = jax.ShapeDtypeStruct(momentum.shape, f32)
    kernel = lambda *refs: update_kernel(span, local_rows, n_ex, *refs)
    return pl.pallas_call(
        kernel,
        grid=(mats, local_rows // rows),
        out_shape=(result, result),
        in_specs=[
            scalar, scalar, block, block, block,
            pl.BlockSpec((2, 1, PART, HALF), lambda k, i: (0, k, 0, 0)),
            pl.BlockSpec((2, 1, PART, HALF), lambda k, i: (0, (k % n_y) * 2 + k // n_y, 0, 0)),
        ],
        out_specs=[block, block],
        compiler_params=pltpu.CompilerParams(vmem_limit_bytes=40 * 2**20),
        name="update",
    )(logit_max, clip_flag, momentum, gradient, weights, part_a, part_b)


def solution(mesh):
    n_dp, n_ex = mesh.shape["dp"], mesh.shape["expert"]

    def body(momentum, gradient, weights, logit_max, clip_flag):
        part_a, part_b = exchange(momentum, gradient, n_dp, n_ex)
        return update(
            momentum, gradient, weights, logit_max, clip_flag, part_a, part_b, n_ex
        )

    spec = P(None, ("dp", "expert"), None)
    return jax.shard_map(
        body,
        mesh=mesh,
        in_specs=(spec, spec, spec, P(), P()),
        out_specs=(spec, spec),
        check_vma=False,
    )
```

```python
import math

import jax
import jax.numpy as jnp
from jax import lax
from jax.experimental import pallas as pl
from jax.experimental.pallas import tpu as pltpu
from jax.sharding import PartitionSpec as P

HEADS = 64
NOPE = 128
VDIM = 128
LATENT = 512
ITERS = 3
ROWS = 16384

momentum_decay = 0.95
learn_rate = 0.2
weight_decay = 0.1
epsilon = 1e-07
clip_tau = 100.0
coeff_a = 3.4445
coeff_b = -4.775
coeff_c = 2.0315

MESH = pl.DeviceIdType.MESH
f32 = jnp.float32
bf16 = jnp.bfloat16
HALF = LATENT // 2
PACK = 3 * HALF
SHARE = PACK // 2
PART = SHARE // 2
CHUNKS = 8
PIECE = SHARE // CHUNKS


def halves(value):
    high = value.astype(bf16)
    return high, (value - high.astype(f32)).astype(bf16)


def dot(left, right):
    return jnp.dot(left, right, preferred_element_type=f32)


def dot_t(left, right):
    return lax.dot_general(left, right, (((1,), (1,)), ((), ())), preferred_element_type=f32)


def dot3(left, right, dot=dot):
    return dot(left[0], right[0]) + (dot(left[0], right[1]) + dot(left[1], right[0]))


def flipped(index, weight):
    bit = (index // weight) % 2
    return index + weight * (1 - 2 * bit), bit


def chain(gsum, ga, gb, q_ref, hi, lo):
    row = lax.broadcasted_iota(jnp.int32, (HALF, HALF), 0)
    col = lax.broadcasted_iota(jnp.int32, (HALF, HALF), 1)
    eye = (row == col).astype(f32)
    g00 = gsum[0:HALF]
    g01 = gsum[HALF : 2 * HALF]
    g11 = gsum[2 * HALF : PACK]
    squares = jnp.sum((g00 + g11) * eye, keepdims=True)
    inverse = 1.0 / (jnp.sqrt(squares) + epsilon)
    inv2 = inverse * inverse

    def put(slot, rows, cols, value):
        high, low = halves(value)
        hi[slot, rows, cols] = high
        lo[slot, rows, cols] = low

    first, second = slice(0, HALF), slice(HALF, LATENT)
    whole = slice(0, LATENT)
    g01 = g01 * inv2
    for rows, cols, value in (
        (first, first, g00 * inv2),
        (first, second, g01),
        (second, first, g01.T),
        (second, second, g11 * inv2),
    ):
        ga[rows, cols] = value
        put(0, rows, cols, value)

    def times(left, right, cols):
        return dot3((hi[left], lo[left]), (hi[right, :, cols], lo[right, :, cols]))

    row = lax.broadcasted_iota(jnp.int32, (LATENT, HALF), 0)
    col = lax.broadcasted_iota(jnp.int32, (LATENT, HALF), 1)
    diagonal = {0: (row == col).astype(f32) * coeff_a, 1: (row == col + HALF).astype(f32) * coeff_a}
    for step in range(ITERS):
        factor_slot = 3 if step == 0 else 1
        for index, cols in enumerate((first, second)):
            factor = diagonal[index] + coeff_b * ga[:, cols] + coeff_c * times(0, 0, cols)
            put(factor_slot, whole, cols, factor)
        if step + 1 < ITERS:
            for cols in (first, second):
                put(2, whole, cols, times(0, factor_slot, cols))
            for cols in (first, second):
                value = times(factor_slot, 2, cols)
                ga[:, cols] = value
                put(0, whole, cols, value)
        if 0 < step < ITERS - 1:
            for cols in (first, second):
                gb[:, cols] = times(3, 1, cols)
            for cols in (first, second):
                put(3, whole, cols, gb[:, cols])
    q_ref[0:HALF] = inverse * dot3((hi[3, first], lo[3, first]), (hi[1, :, first], lo[1, :, first]))
    right = times(3, 1, second)
    q_ref[HALF:PACK] = inverse * right


def exchange_kernel(
    n_dp, n_ex, m_any, g_any, out_a, out_b,
    m_buf, g_buf, gram, from_core, buf, rec,
    z_own, z_left, z_right, s_left, s_right, gsum, packed, ga, gb, hi, lo,
    load_sem, core_send, core_recv, plane_send, plane_recv, z_send, z_recv, sum_send, sum_recv,
    back_send, back_recv,
):
    mats = m_buf.shape[0]
    n_y = n_ex // 2
    steps = mats.bit_length() - 1
    d, e = lax.axis_index("dp"), lax.axis_index("expert")
    mate, core = flipped(e, 1)
    other_x, x_bit = flipped(d, 1)
    here, line = d // 2, n_dp // 2
    y = e // 2

    for k in range(mats):
        pltpu.make_async_copy(m_any.at[k], m_buf.at[k], load_sem.at[k, 0]).start()
        pltpu.make_async_copy(g_any.at[k], g_buf.at[k], load_sem.at[k, 1]).start()

    y_bits = []
    weight = n_y // 2
    while weight >= 1:
        partner, bit = flipped(e, 2 * weight)
        y_bits.append(({"expert": partner}, bit))
        weight //= 2
    x_entry = ({"dp": other_x}, x_bit)
    order_a, order_b = [x_entry] + y_bits, y_bits + [x_entry]

    barrier = pltpu.get_barrier_semaphore()
    pl.semaphore_signal(barrier, inc=1, device_id={"expert": mate}, device_id_type=MESH)
    for partner, _ in order_a:
        pl.semaphore_signal(barrier, inc=1, device_id=partner, device_id_type=MESH)

    @pl.when(here > 0)
    def _():
        pl.semaphore_signal(barrier, inc=1, device_id={"dp": d - 2}, device_id_type=MESH)

    @pl.when(here < line - 1)
    def _():
        pl.semaphore_signal(barrier, inc=1, device_id={"dp": d + 2}, device_id_type=MESH)

    ends = (here > 0).astype(jnp.int32) + (here < line - 1).astype(jnp.int32)
    pl.semaphore_wait(barrier, 1 + steps + ends)

    def core_copy(k):
        return pltpu.make_async_remote_copy(
            src_ref=gram.at[k, pl.ds((1 - core) * SHARE, SHARE)],
            dst_ref=from_core.at[k],
            send_sem=core_send.at[k],
            recv_sem=core_recv.at[k],
            device_id={"expert": mate},
            device_id_type=MESH,
        )

    @pl.loop(0, mats)
    def _(k):
        pltpu.make_async_copy(m_any.at[k], m_buf.at[k], load_sem.at[k, 0]).wait()
        pltpu.make_async_copy(g_any.at[k], g_buf.at[k], load_sem.at[k, 1]).wait()
        moved = momentum_decay * m_buf[k] + g_buf[k].astype(f32)
        high, low = halves(moved)
        high_t, low_t = halves(moved.T)
        for at, (i, j) in enumerate(((0, 0), (0, 1), (1, 1))):
            rows, cols = slice(i * HALF, (i + 1) * HALF), slice(j * HALF, (j + 1) * HALF)
            gram[k, at * HALF : (at + 1) * HALF] = dot3(
                (high_t[rows], low_t[rows]), (high[:, cols], low[:, cols])
            )
        core_copy(k).start()

    @pl.loop(0, mats)
    def _(k):
        core_copy(k).wait()
        swapped = (k % n_y) * 2 + k // n_y
        start = pl.multiple_of(core * SHARE, SHARE)
        for c in range(CHUNKS):
            own = gram[k, pl.ds(start + c * PIECE, PIECE)]
            buf[c, k if c % 2 == 0 else swapped] = own + from_core[k, c * PIECE : (c + 1) * PIECE]

    def pick(side, first, second):
        return first + side * (second - first)

    def target_of(partner):
        return partner.get("dp", d), partner.get("expert", e)

    def route(c, step):
        side = c % 2
        at, count = 0, mats
        for i in range(step + 1):
            bit = pick(side, order_a[i][1], order_b[i][1])
            if i < step:
                count //= 2
                at = at + bit * count
        first, second = target_of(order_a[step][0]), target_of(order_b[step][0])
        partner = (pick(side, first[0], second[0]), pick(side, first[1], second[1]))
        return at, count // 2, bit, partner

    def plane_copies(c, step):
        at, count, bit, partner = route(c, step)
        offset = mats - 2 * count
        source = at + (1 - bit) * count
        if step + 1 < steps:
            half = count // 2
            next_bit = pick(c % 2, order_a[step + 1][1], order_b[step + 1][1])
            spans = [(0, (1 - next_bit) * half, half), (1, next_bit * half, half)]
        else:
            spans = [(0, 0, count)]
        return [
            pltpu.make_async_remote_copy(
                src_ref=buf.at[c, pl.ds(source + shift, size)],
                dst_ref=rec.at[c, pl.ds(offset + shift, size)],
                send_sem=plane_send.at[step, i, c],
                recv_sem=plane_recv.at[step, i, c],
                device_id=partner,
                device_id_type=MESH,
            )
            for i, shift, size in spans
        ]

    def take(c, step):
        at, count, bit, _ = route(c, step)
        offset = mats - 2 * count
        keep = at + bit * count
        copies = plane_copies(c, step)
        if step + 1 < steps:
            half = count // 2
            next_bit = pick(c % 2, order_a[step + 1][1], order_b[step + 1][1])
            shifts = [(1 - next_bit) * half, next_bit * half]
        else:
            half, shifts = count, [0]
        for i, shift in enumerate(shifts):
            copies[i].wait_recv()
            for j in range(half):
                total = buf[c, keep + shift + j] + rec[c, offset + shift + j]
                if step + 1 < steps:
                    buf[c, keep + shift + j] = total
                else:
                    z_own[c] = total
            if i == 0 and step + 1 < steps:
                for copy in plane_copies(c, step + 1):
                    copy.start()

    @pl.loop(0, CHUNKS)
    def _(c):
        for copy in plane_copies(c, 0):
            copy.start()

    at_a = at_b = 0
    for step in range(steps):
        at_a = at_a + order_a[step][1] * (mats >> (step + 1))
        at_b = at_b + order_b[step][1] * (mats >> (step + 1))

    @pl.when(here == 0)
    def _():
        z_left[...] = jnp.zeros_like(z_left)

    @pl.when(here == line - 1)
    def _():
        z_right[...] = jnp.zeros_like(z_right)

    def line_copy(way, c):
        source, target = ((s_left, z_left), (s_right, z_right))[way]
        return pltpu.make_async_remote_copy(
            src_ref=source.at[c],
            dst_ref=target.at[c],
            send_sem=z_send.at[way, c],
            recv_sem=z_recv.at[way, c],
            device_id={"dp": d + 2 if way == 0 else d - 2},
            device_id_type=MESH,
        )

    def sum_copy(c):
        rows = pl.ds(pl.multiple_of(core * SHARE + c * PIECE, PIECE), PIECE)
        return pltpu.make_async_remote_copy(
            src_ref=gsum.at[rows],
            dst_ref=gsum.at[rows],
            send_sem=sum_send.at[c],
            recv_sem=sum_recv.at[c],
            device_id={"expert": mate},
            device_id_type=MESH,
        )

    there = line - 1 - here
    far = jnp.maximum(here, there)

    lag = steps - 1

    @pl.loop(0, line + CHUNKS - 1 + lag)
    def _(u):
        for step in range(steps):

            @pl.when((u >= step) & (u - step < CHUNKS))
            def _():
                take(u - step, step)

        t = u - lag
        for way, behind in ((0, here), (1, there)):
            source, target = ((s_left, z_left), (s_right, z_right))[way]
            c = t - behind

            @pl.when((c >= 0) & (c < CHUNKS))
            def _():
                @pl.when(behind > 0)
                def _():
                    line_copy(way, c).wait_recv()

                @pl.when(behind < line - 1)
                def _():
                    source[c] = target[c] + z_own[c]
                    line_copy(way, c).start()

        c = t - far

        @pl.when((c >= 0) & (c < CHUNKS))
        def _():
            rows = pl.ds(pl.multiple_of(core * SHARE + c * PIECE, PIECE), PIECE)
            gsum[rows] = (z_left[c] + z_own[c]) + z_right[c]
            sum_copy(c).start()

    @pl.loop(0, CHUNKS)
    def _(c):
        sum_copy(c).wait()
        for step in range(steps):
            for copy in plane_copies(c, step):
                copy.wait_send()

        @pl.when(here < line - 1)
        def _():
            line_copy(0, c).wait_send()

        @pl.when(here > 0)
        def _():
            line_copy(1, c).wait_send()

    chain(gsum, ga, gb, packed, hi, lo)

    sides = []
    for buf_out, at, order, odd in ((out_a, at_a, order_a, 0), (out_b, at_b, order_b, 1)):
        for q in range(CHUNKS // 2):
            rows = pl.multiple_of(core * SHARE + (2 * q + odd) * PIECE, PIECE)
            buf_out[core, at, q * PIECE : (q + 1) * PIECE] = packed[pl.ds(rows, PIECE)]
        back = order[::-1]
        sides.append((buf_out, at, back, odd))

    def back_copy(side, step, block):
        buf_out, at, back, odd = sides[side]
        slot = at
        for i in range(steps):
            if (block >> i) % 2:
                slot = slot + (1 - 2 * back[i][1]) * (1 << i)
        ref = buf_out.at[core, slot]
        return pltpu.make_async_remote_copy(
            src_ref=ref,
            dst_ref=ref,
            send_sem=back_send.at[side, (1 << step) - 1 + block],
            recv_sem=back_recv.at[side, (1 << step) - 1 + block],
            device_id=back[step][0] if step < steps else {"expert": mate},
            device_id_type=MESH,
        )

    for block in range(mats):
        for side in range(2):
            if block > 0:
                top = block.bit_length() - 1
                back_copy(side, top, block - (1 << top)).wait_recv()
            for step in range(steps, -1, -1):
                if (1 << step) > block:
                    back_copy(side, step, block).start()
    for block in range(mats):
        for side in range(2):
            back_copy(side, steps, block).wait_recv()
    for step in range(steps + 1):
        for block in range(1 << step):
            for side in range(2):
                back_copy(side, step, block).wait_send()


def exchange(momentum, gradient, n_dp, n_ex):
    mats, rows, width = momentum.shape
    steps = mats.bit_length() - 1
    dma = pltpu.SemaphoreType.DMA
    kernel = lambda *refs: exchange_kernel(n_dp, n_ex, *refs)
    result = jax.ShapeDtypeStruct((2, mats, PART, HALF), f32)
    return pl.pallas_call(
        kernel,
        out_shape=(result, result),
        in_specs=[pl.BlockSpec(memory_space=pl.ANY)] * 2,
        out_specs=[pl.BlockSpec(memory_space=pltpu.VMEM)] * 2,
        scratch_shapes=[
            pltpu.VMEM((mats, rows, width), f32),
            pltpu.VMEM((mats, rows, width), bf16),
            pltpu.VMEM((mats, PACK, HALF), f32),
            pltpu.VMEM((mats, SHARE, HALF), f32),
            pltpu.VMEM((CHUNKS, mats, PIECE, HALF), f32),
            pltpu.VMEM((CHUNKS, mats, PIECE, HALF), f32),
        ]
        + [pltpu.VMEM((CHUNKS, PIECE, HALF), f32)] * 5
        + [pltpu.VMEM((PACK, HALF), f32)] * 2
        + [pltpu.VMEM((width, width), f32)] * 2
        + [pltpu.VMEM((4, width, width), bf16)] * 2
        + [dma((mats, 2)), dma((mats,)), dma((mats,))]
        + [dma((steps, 2, CHUNKS))] * 2
        + [dma((2, CHUNKS))] * 2
        + [dma((CHUNKS,))] * 2
        + [dma((2, 2 * mats - 1))] * 2,
        compiler_params=pltpu.CompilerParams(
            collective_id=0, has_side_effects=True, vmem_limit_bytes=32 * 2**20
        ),
        name="exchange",
    )(momentum, gradient)


def update_kernel(
    span, local_rows, n_ex, logit_ref, flag_ref, m_ref, g_ref, w_ref, a_ref, b_ref, w_out, m_out,
):
    k, tile = pl.program_id(0), pl.program_id(1)
    rows = m_ref.shape[1]
    moved = momentum_decay * m_ref[0] + g_ref[0].astype(f32)
    m_out[0] = moved
    high, low = halves(moved)
    pack = jnp.concatenate(
        [
            ref[core, 0, q * PIECE : (q + 1) * PIECE]
            for core in range(2)
            for q in range(CHUNKS // 2)
            for ref in (a_ref, b_ref)
        ],
        axis=0,
    )
    pack_hi, pack_lo = halves(pack)
    p00, p01, p11 = [
        (pack_hi[i * HALF : (i + 1) * HALF], pack_lo[i * HALF : (i + 1) * HALF]) for i in range(3)
    ]
    x0 = (high[:, :HALF], low[:, :HALF])
    x1 = (high[:, HALF:], low[:, HALF:])
    ortho = (dot3(x0, p00) + dot3(x1, p01, dot_t), dot3(x0, p01) + dot3(x1, p11))
    update_scale = 0.2 * math.sqrt(max(ROWS, LATENT))
    first = (lax.axis_index("dp") * n_ex + lax.axis_index("expert")) * local_rows + tile * rows
    for i in range(rows // span):
        row = first + i * span
        head = row // (NOPE + VDIM)
        logit = jnp.full((1, HALF), logit_ref[k, head], jnp.int32).astype(f32)
        use = jnp.full((1, HALF), flag_ref[k, head], jnp.int32) == 1
        keyed = jnp.full((1, HALF), row % (NOPE + VDIM), jnp.int32) < NOPE
        root = jnp.sqrt(jnp.minimum(1.0, clip_tau / logit))
        factor = jnp.where(use & keyed, root, 1.0)
        at = slice(i * span, (i + 1) * span)
        for j in range(2):
            cols = slice(j * HALF, (j + 1) * HALF)
            weight = w_ref[0, at, cols]
            stepped = weight - learn_rate * (
                update_scale * ortho[j][at] + weight_decay * weight
            )
            w_out[0, at, cols] = stepped * factor


def update(momentum, gradient, weights, logit_max, clip_flag, part_a, part_b, n_ex):
    mats, local_rows, width = momentum.shape
    rows = min(local_rows, 256)
    span = min(rows, NOPE)
    n_y = n_ex // 2
    block = pl.BlockSpec((1, rows, width), lambda k, i: (k, i, 0))
    scalar = pl.BlockSpec(memory_space=pltpu.SMEM)
    result = jax.ShapeDtypeStruct(momentum.shape, f32)
    kernel = lambda *refs: update_kernel(span, local_rows, n_ex, *refs)
    return pl.pallas_call(
        kernel,
        grid=(mats, local_rows // rows),
        out_shape=(result, result),
        in_specs=[
            scalar, scalar, block, block, block,
            pl.BlockSpec((2, 1, PART, HALF), lambda k, i: (0, k, 0, 0)),
            pl.BlockSpec((2, 1, PART, HALF), lambda k, i: (0, (k % n_y) * 2 + k // n_y, 0, 0)),
        ],
        out_specs=[block, block],
        compiler_params=pltpu.CompilerParams(vmem_limit_bytes=20 * 2**20),
        name="update",
    )(logit_max, clip_flag, momentum, gradient, weights, part_a, part_b)


def solution(mesh):
    n_dp, n_ex = mesh.shape["dp"], mesh.shape["expert"]

    def body(momentum, gradient, weights, logit_max, clip_flag):
        part_a, part_b = exchange(momentum, gradient, n_dp, n_ex)
        return update(
            momentum, gradient, weights, logit_max, clip_flag, part_a, part_b, n_ex
        )

    spec = P(None, ("dp", "expert"), None)
    return jax.shard_map(
        body,
        mesh=mesh,
        in_specs=(spec, spec, spec, P(), P()),
        out_specs=(spec, spec),
        check_vma=False,
    )
```

```python
import math

import jax
import jax.numpy as jnp
from jax import lax
from jax.experimental import pallas as pl
from jax.experimental.pallas import tpu as pltpu
from jax.sharding import PartitionSpec as P

HEADS = 64
NOPE = 128
VDIM = 128
LATENT = 512
ITERS = 3
ROWS = 16384

momentum_decay = 0.95
learn_rate = 0.2
weight_decay = 0.1
epsilon = 1e-07
clip_tau = 100.0
coeff_a = 3.4445
coeff_b = -4.775
coeff_c = 2.0315

MESH = pl.DeviceIdType.MESH
f32 = jnp.float32
bf16 = jnp.bfloat16
HALF = LATENT // 2
PACK = 3 * HALF
SHARE = PACK // 2
PART = SHARE // 2
CHUNKS = 4
PIECE = SHARE // CHUNKS


def halves(value):
    high = value.astype(bf16)
    return high, (value - high.astype(f32)).astype(bf16)


def dot(left, right):
    return jnp.dot(left, right, preferred_element_type=f32)


def dot_t(left, right):
    return lax.dot_general(left, right, (((1,), (1,)), ((), ())), preferred_element_type=f32)


def dot3(left, right, dot=dot):
    return dot(left[0], right[0]) + (dot(left[0], right[1]) + dot(left[1], right[0]))


def flipped(index, weight):
    bit = (index // weight) % 2
    return index + weight * (1 - 2 * bit), bit


def chain(gsum, ga, gb, q_ref, hi, lo):
    row = lax.broadcasted_iota(jnp.int32, (HALF, HALF), 0)
    col = lax.broadcasted_iota(jnp.int32, (HALF, HALF), 1)
    eye = (row == col).astype(f32)
    g00 = gsum[0:HALF]
    g01 = gsum[HALF : 2 * HALF]
    g11 = gsum[2 * HALF : PACK]
    squares = jnp.sum((g00 + g11) * eye, keepdims=True)
    inverse = 1.0 / (jnp.sqrt(squares) + epsilon)
    inv2 = inverse * inverse

    def put(slot, rows, cols, value):
        high, low = halves(value)
        hi[slot, rows, cols] = high
        lo[slot, rows, cols] = low

    first, second = slice(0, HALF), slice(HALF, LATENT)
    whole = slice(0, LATENT)
    g01 = g01 * inv2
    for rows, cols, value in (
        (first, first, g00 * inv2),
        (first, second, g01),
        (second, first, g01.T),
        (second, second, g11 * inv2),
    ):
        ga[rows, cols] = value
        put(0, rows, cols, value)

    def times(left, right, cols):
        return dot3((hi[left], lo[left]), (hi[right, :, cols], lo[right, :, cols]))

    row = lax.broadcasted_iota(jnp.int32, (LATENT, HALF), 0)
    col = lax.broadcasted_iota(jnp.int32, (LATENT, HALF), 1)
    diagonal = {0: (row == col).astype(f32) * coeff_a, 1: (row == col + HALF).astype(f32) * coeff_a}
    for step in range(ITERS):
        factor_slot = 3 if step == 0 else 1
        for index, cols in enumerate((first, second)):
            factor = diagonal[index] + coeff_b * ga[:, cols] + coeff_c * times(0, 0, cols)
            put(factor_slot, whole, cols, factor)
        if step + 1 < ITERS:
            for cols in (first, second):
                put(2, whole, cols, times(0, factor_slot, cols))
            for cols in (first, second):
                value = times(factor_slot, 2, cols)
                ga[:, cols] = value
                put(0, whole, cols, value)
        if 0 < step < ITERS - 1:
            for cols in (first, second):
                gb[:, cols] = times(3, 1, cols)
            for cols in (first, second):
                put(3, whole, cols, gb[:, cols])
    q_ref[0:HALF] = inverse * dot3((hi[3, first], lo[3, first]), (hi[1, :, first], lo[1, :, first]))
    right = times(3, 1, second)
    q_ref[HALF:PACK] = inverse * right


def exchange_kernel(
    n_dp, n_ex, m_any, g_any, out_a, out_b,
    m_buf, g_buf, gram, from_core, buf, rec,
    z_own, z_left, z_right, s_left, s_right, gsum, packed, ga, gb, hi, lo,
    load_sem, core_send, core_recv, plane_send, plane_recv, z_send, z_recv, sum_send, sum_recv,
    back_send, back_recv,
):
    mats = m_buf.shape[0]
    n_y = n_ex // 2
    steps = mats.bit_length() - 1
    d, e = lax.axis_index("dp"), lax.axis_index("expert")
    mate, core = flipped(e, 1)
    other_x, x_bit = flipped(d, 1)
    here, line = d // 2, n_dp // 2
    y = e // 2

    for k in range(mats):
        pltpu.make_async_copy(m_any.at[k], m_buf.at[k], load_sem.at[k, 0]).start()
        pltpu.make_async_copy(g_any.at[k], g_buf.at[k], load_sem.at[k, 1]).start()

    y_bits = []
    weight = n_y // 2
    while weight >= 1:
        partner, bit = flipped(e, 2 * weight)
        y_bits.append(({"expert": partner}, bit))
        weight //= 2
    x_entry = ({"dp": other_x}, x_bit)
    order_a, order_b = [x_entry] + y_bits, y_bits + [x_entry]

    barrier = pltpu.get_barrier_semaphore()
    pl.semaphore_signal(barrier, inc=1, device_id={"expert": mate}, device_id_type=MESH)
    for partner, _ in order_a:
        pl.semaphore_signal(barrier, inc=1, device_id=partner, device_id_type=MESH)

    @pl.when(here > 0)
    def _():
        pl.semaphore_signal(barrier, inc=1, device_id={"dp": d - 2}, device_id_type=MESH)

    @pl.when(here < line - 1)
    def _():
        pl.semaphore_signal(barrier, inc=1, device_id={"dp": d + 2}, device_id_type=MESH)

    ends = (here > 0).astype(jnp.int32) + (here < line - 1).astype(jnp.int32)
    pl.semaphore_wait(barrier, 1 + steps + ends)

    def core_copy(k):
        return pltpu.make_async_remote_copy(
            src_ref=gram.at[k, pl.ds((1 - core) * SHARE, SHARE)],
            dst_ref=from_core.at[k],
            send_sem=core_send.at[k],
            recv_sem=core_recv.at[k],
            device_id={"expert": mate},
            device_id_type=MESH,
        )

    @pl.loop(0, mats)
    def _(k):
        pltpu.make_async_copy(m_any.at[k], m_buf.at[k], load_sem.at[k, 0]).wait()
        pltpu.make_async_copy(g_any.at[k], g_buf.at[k], load_sem.at[k, 1]).wait()
        moved = momentum_decay * m_buf[k] + g_buf[k].astype(f32)
        high, low = halves(moved)
        high_t, low_t = halves(moved.T)
        for at, (i, j) in enumerate(((0, 0), (0, 1), (1, 1))):
            rows, cols = slice(i * HALF, (i + 1) * HALF), slice(j * HALF, (j + 1) * HALF)
            gram[k, at * HALF : (at + 1) * HALF] = dot3(
                (high_t[rows], low_t[rows]), (high[:, cols], low[:, cols])
            )
        core_copy(k).start()

    @pl.loop(0, mats)
    def _(k):
        core_copy(k).wait()
        swapped = (k % n_y) * 2 + k // n_y
        start = pl.multiple_of(core * SHARE, SHARE)
        for c in range(CHUNKS):
            own = gram[k, pl.ds(start + c * PIECE, PIECE)]
            buf[c, k if c % 2 == 0 else swapped] = own + from_core[k, c * PIECE : (c + 1) * PIECE]

    def pick(side, first, second):
        return first + side * (second - first)

    def target_of(partner):
        return partner.get("dp", d), partner.get("expert", e)

    def route(c, step):
        side = c % 2
        at, count = 0, mats
        for i in range(step + 1):
            bit = pick(side, order_a[i][1], order_b[i][1])
            if i < step:
                count //= 2
                at = at + bit * count
        first, second = target_of(order_a[step][0]), target_of(order_b[step][0])
        partner = (pick(side, first[0], second[0]), pick(side, first[1], second[1]))
        return at, count // 2, bit, partner

    def plane_copies(c, step):
        at, count, bit, partner = route(c, step)
        offset = mats - 2 * count
        source = at + (1 - bit) * count
        if step + 1 < steps:
            half = count // 2
            next_bit = pick(c % 2, order_a[step + 1][1], order_b[step + 1][1])
            spans = [(0, (1 - next_bit) * half, half), (1, next_bit * half, half)]
        else:
            spans = [(0, 0, count)]
        return [
            pltpu.make_async_remote_copy(
                src_ref=buf.at[c, pl.ds(source + shift, size)],
                dst_ref=rec.at[c, pl.ds(offset + shift, size)],
                send_sem=plane_send.at[step, i, c],
                recv_sem=plane_recv.at[step, i, c],
                device_id=partner,
                device_id_type=MESH,
            )
            for i, shift, size in spans
        ]

    def take(c, step):
        at, count, bit, _ = route(c, step)
        offset = mats - 2 * count
        keep = at + bit * count
        copies = plane_copies(c, step)
        if step + 1 < steps:
            half = count // 2
            next_bit = pick(c % 2, order_a[step + 1][1], order_b[step + 1][1])
            shifts = [(1 - next_bit) * half, next_bit * half]
        else:
            half, shifts = count, [0]
        for i, shift in enumerate(shifts):
            copies[i].wait_recv()
            for j in range(half):
                total = buf[c, keep + shift + j] + rec[c, offset + shift + j]
                if step + 1 < steps:
                    buf[c, keep + shift + j] = total
                else:
                    z_own[c] = total
            if i == 0 and step + 1 < steps:
                for copy in plane_copies(c, step + 1):
                    copy.start()

    @pl.loop(0, CHUNKS)
    def _(c):
        for copy in plane_copies(c, 0):
            copy.start()

    at_a = at_b = 0
    for step in range(steps):
        at_a = at_a + order_a[step][1] * (mats >> (step + 1))
        at_b = at_b + order_b[step][1] * (mats >> (step + 1))

    @pl.when(here == 0)
    def _():
        z_left[...] = jnp.zeros_like(z_left)

    @pl.when(here == line - 1)
    def _():
        z_right[...] = jnp.zeros_like(z_right)

    def line_copy(way, c):
        source, target = ((s_left, z_left), (s_right, z_right))[way]
        return pltpu.make_async_remote_copy(
            src_ref=source.at[c],
            dst_ref=target.at[c],
            send_sem=z_send.at[way, c],
            recv_sem=z_recv.at[way, c],
            device_id={"dp": d + 2 if way == 0 else d - 2},
            device_id_type=MESH,
        )

    def sum_copy(c):
        rows = pl.ds(pl.multiple_of(core * SHARE + c * PIECE, PIECE), PIECE)
        return pltpu.make_async_remote_copy(
            src_ref=gsum.at[rows],
            dst_ref=gsum.at[rows],
            send_sem=sum_send.at[c],
            recv_sem=sum_recv.at[c],
            device_id={"expert": mate},
            device_id_type=MESH,
        )

    there = line - 1 - here
    far = jnp.maximum(here, there)

    lag = steps - 1

    @pl.loop(0, line + CHUNKS - 1 + lag)
    def _(u):
        for step in range(steps):

            @pl.when((u >= step) & (u - step < CHUNKS))
            def _():
                take(u - step, step)

        t = u - lag
        for way, behind in ((0, here), (1, there)):
            source, target = ((s_left, z_left), (s_right, z_right))[way]
            c = t - behind

            @pl.when((c >= 0) & (c < CHUNKS))
            def _():
                @pl.when(behind > 0)
                def _():
                    line_copy(way, c).wait_recv()

                @pl.when(behind < line - 1)
                def _():
                    source[c] = target[c] + z_own[c]
                    line_copy(way, c).start()

        c = t - far

        @pl.when((c >= 0) & (c < CHUNKS))
        def _():
            rows = pl.ds(pl.multiple_of(core * SHARE + c * PIECE, PIECE), PIECE)
            gsum[rows] = (z_left[c] + z_own[c]) + z_right[c]
            sum_copy(c).start()

    @pl.loop(0, CHUNKS)
    def _(c):
        sum_copy(c).wait()
        for step in range(steps):
            for copy in plane_copies(c, step):
                copy.wait_send()

        @pl.when(here < line - 1)
        def _():
            line_copy(0, c).wait_send()

        @pl.when(here > 0)
        def _():
            line_copy(1, c).wait_send()

    chain(gsum, ga, gb, packed, hi, lo)

    sides = []
    for buf_out, at, order, odd in ((out_a, at_a, order_a, 0), (out_b, at_b, order_b, 1)):
        for q in range(CHUNKS // 2):
            rows = pl.multiple_of(core * SHARE + (2 * q + odd) * PIECE, PIECE)
            buf_out[core, at, q * PIECE : (q + 1) * PIECE] = packed[pl.ds(rows, PIECE)]
        back = order[::-1]
        sides.append((buf_out, at, back, odd))

    def back_copy(side, step, block):
        buf_out, at, back, odd = sides[side]
        slot = at
        for i in range(steps):
            if (block >> i) % 2:
                slot = slot + (1 - 2 * back[i][1]) * (1 << i)
        ref = buf_out.at[core, slot]
        return pltpu.make_async_remote_copy(
            src_ref=ref,
            dst_ref=ref,
            send_sem=back_send.at[side, (1 << step) - 1 + block],
            recv_sem=back_recv.at[side, (1 << step) - 1 + block],
            device_id=back[step][0] if step < steps else {"expert": mate},
            device_id_type=MESH,
        )

    for block in range(mats):
        for side in range(2):
            if block > 0:
                top = block.bit_length() - 1
                back_copy(side, top, block - (1 << top)).wait_recv()
            for step in range(steps, -1, -1):
                if (1 << step) > block:
                    back_copy(side, step, block).start()
    for block in range(mats):
        for side in range(2):
            back_copy(side, steps, block).wait_recv()
    for step in range(steps + 1):
        for block in range(1 << step):
            for side in range(2):
                back_copy(side, step, block).wait_send()


def exchange(momentum, gradient, n_dp, n_ex):
    mats, rows, width = momentum.shape
    steps = mats.bit_length() - 1
    dma = pltpu.SemaphoreType.DMA
    kernel = lambda *refs: exchange_kernel(n_dp, n_ex, *refs)
    result = jax.ShapeDtypeStruct((2, mats, PART, HALF), f32)
    return pl.pallas_call(
        kernel,
        out_shape=(result, result),
        in_specs=[pl.BlockSpec(memory_space=pl.ANY)] * 2,
        out_specs=[pl.BlockSpec(memory_space=pltpu.VMEM)] * 2,
        scratch_shapes=[
            pltpu.VMEM((mats, rows, width), f32),
            pltpu.VMEM((mats, rows, width), bf16),
            pltpu.VMEM((mats, PACK, HALF), f32),
            pltpu.VMEM((mats, SHARE, HALF), f32),
            pltpu.VMEM((CHUNKS, mats, PIECE, HALF), f32),
            pltpu.VMEM((CHUNKS, mats, PIECE, HALF), f32),
        ]
        + [pltpu.VMEM((CHUNKS, PIECE, HALF), f32)] * 5
        + [pltpu.VMEM((PACK, HALF), f32)] * 2
        + [pltpu.VMEM((width, width), f32)] * 2
        + [pltpu.VMEM((4, width, width), bf16)] * 2
        + [dma((mats, 2)), dma((mats,)), dma((mats,))]
        + [dma((steps, 2, CHUNKS))] * 2
        + [dma((2, CHUNKS))] * 2
        + [dma((CHUNKS,))] * 2
        + [dma((2, 2 * mats - 1))] * 2,
        compiler_params=pltpu.CompilerParams(
            collective_id=0, has_side_effects=True, vmem_limit_bytes=32 * 2**20
        ),
        name="exchange",
    )(momentum, gradient)


def update_kernel(
    span, local_rows, n_ex, logit_ref, flag_ref, m_ref, g_ref, w_ref, a_ref, b_ref, w_out, m_out,
):
    k, tile = pl.program_id(0), pl.program_id(1)
    rows = m_ref.shape[1]
    moved = momentum_decay * m_ref[0] + g_ref[0].astype(f32)
    m_out[0] = moved
    high, low = halves(moved)
    pack = jnp.concatenate(
        [
            ref[core, 0, q * PIECE : (q + 1) * PIECE]
            for core in range(2)
            for q in range(CHUNKS // 2)
            for ref in (a_ref, b_ref)
        ],
        axis=0,
    )
    pack_hi, pack_lo = halves(pack)
    p00, p01, p11 = [
        (pack_hi[i * HALF : (i + 1) * HALF], pack_lo[i * HALF : (i + 1) * HALF]) for i in range(3)
    ]
    x0 = (high[:, :HALF], low[:, :HALF])
    x1 = (high[:, HALF:], low[:, HALF:])
    ortho = (dot3(x0, p00) + dot3(x1, p01, dot_t), dot3(x0, p01) + dot3(x1, p11))
    update_scale = 0.2 * math.sqrt(max(ROWS, LATENT))
    first = (lax.axis_index("dp") * n_ex + lax.axis_index("expert")) * local_rows + tile * rows
    for i in range(rows // span):
        row = first + i * span
        head = row // (NOPE + VDIM)
        logit = jnp.full((1, HALF), logit_ref[k, head], jnp.int32).astype(f32)
        use = jnp.full((1, HALF), flag_ref[k, head], jnp.int32) == 1
        keyed = jnp.full((1, HALF), row % (NOPE + VDIM), jnp.int32) < NOPE
        root = jnp.sqrt(jnp.minimum(1.0, clip_tau / logit))
        factor = jnp.where(use & keyed, root, 1.0)
        at = slice(i * span, (i + 1) * span)
        for j in range(2):
            cols = slice(j * HALF, (j + 1) * HALF)
            weight = w_ref[0, at, cols]
            stepped = weight - learn_rate * (
                update_scale * ortho[j][at] + weight_decay * weight
            )
            w_out[0, at, cols] = stepped * factor


def update(momentum, gradient, weights, logit_max, clip_flag, part_a, part_b, n_ex):
    mats, local_rows, width = momentum.shape
    rows = min(local_rows, 256)
    span = min(rows, NOPE)
    n_y = n_ex // 2
    block = pl.BlockSpec((1, rows, width), lambda k, i: (k, i, 0))
    scalar = pl.BlockSpec(memory_space=pltpu.SMEM)
    result = jax.ShapeDtypeStruct(momentum.shape, f32)
    kernel = lambda *refs: update_kernel(span, local_rows, n_ex, *refs)
    return pl.pallas_call(
        kernel,
        grid=(mats, local_rows // rows),
        out_shape=(result, result),
        in_specs=[
            scalar, scalar, block, block, block,
            pl.BlockSpec((2, 1, PART, HALF), lambda k, i: (0, k, 0, 0)),
            pl.BlockSpec((2, 1, PART, HALF), lambda k, i: (0, (k % n_y) * 2 + k // n_y, 0, 0)),
        ],
        out_specs=[block, block],
        compiler_params=pltpu.CompilerParams(vmem_limit_bytes=20 * 2**20),
        name="update",
    )(logit_max, clip_flag, momentum, gradient, weights, part_a, part_b)


def solution(mesh):
    n_dp, n_ex = mesh.shape["dp"], mesh.shape["expert"]

    def body(momentum, gradient, weights, logit_max, clip_flag):
        part_a, part_b = exchange(momentum, gradient, n_dp, n_ex)
        return update(
            momentum, gradient, weights, logit_max, clip_flag, part_a, part_b, n_ex
        )

    spec = P(None, ("dp", "expert"), None)
    return jax.shard_map(
        body,
        mesh=mesh,
        in_specs=(spec, spec, spec, P(), P()),
        out_specs=(spec, spec),
        check_vma=False,
    )
```
